32 devices in a mesh: section: 4 (over z), fsdp: 8 (over y, x, core).
Axes of the slice: x: 2, y: 2, z: 4, core: 2. Of those that a mesh axis runs over, the one named last changes fastest.
Arguments:
- saved_inputs: bfloat16 [4, 4, 384, 2048], P('section', None, 'fsdp'), may hold values from -6 to 6
- attn_weights: bfloat16 [4, 2048, 4096], P('section', 'fsdp'), may hold values from -16 to 16
- grad_out: bfloat16 [4, 384, 2048], P(None, 'fsdp'), may hold values from -1.1953125 to 1.1953125
- segments: int32 [4, 8, 48], P(None, 'fsdp'), may hold values from 0 to 2, never falling along the last dimension, each value on 1 to 24 neighbouring positions
- coords: float32 [3, 4, 384], P(None, None, 'fsdp'), may hold values from -4 to 4
- embed_in: bfloat16 [2048, 4], P(('section', 'fsdp')), may hold values from -4 to 4
- embed_out: bfloat16 [2048, 2048], P(('section', 'fsdp')), may hold values from -0.125 to 0.125
Outputs:
- attn_grad: float32 [4, 2048, 4096], P('section', 'fsdp')
- input_grad: bfloat16 [4, 384, 2048], P(None, 'fsdp')
- embed_out_grad: float32 [2048, 2048], P(('section', 'fsdp'))
- embed_in_grad: float32 [2048, 4], P(('section', 'fsdp'))
The draws below stay inside these ranges and needn't reach their ends.
Inputs may be any that keep to these rules, and one draw needn't show every extreme that they name: `segments`: sessions never straddle a block of 48 tokens; within a block segment numbers never fall and each session is one run of at most 24 tokens.
All inputs are finite; a program needn't handle non-finite values.
Results may differ from the reference program's by a relative error of at most 0.02.
Values may be sent and summed in bfloat16 or wider, within the bound.
A program may use at most 128 MiB of HBM per device.

```python
import math
import jax
import jax.numpy as jnp
import numpy as np
from jax import lax

D = 2048
HEADS = 16
HEAD_DIM = 64
HID = 2048
ROWS = 48
MICRO = 4
SESS = 3
AW = 1024
LAYERS = 4
BLOCKS = 8
TOKENS = 384
N_FSDP = 8


def draw_attn_weights(key, part):
    attn_width = HEADS * HEAD_DIM
    shape = (LAYERS, D, 4 * attn_width)
    first_key = jax.random.fold_in(key, 11)
    base = jax.random.normal(first_key, shape, jnp.float32)
    column = jnp.arange(4 * attn_width)
    fan = jnp.where(column < 3 * attn_width, D, attn_width).astype(jnp.float32)
    weights = base / jnp.sqrt(fan)[None, None, :]
    return weights.astype(jnp.bfloat16)


def level_of(rng, shape, split, low, top_value):
    factor_of = 1.0
    for position, blocks in split:
        steps = jax.random.uniform(jax.random.fold_in(jax.random.fold_in(rng, 6), position), (blocks,), jnp.float32, low / len(split), top_value / len(split))
        factor_of = factor_of * jnp.repeat(jnp.exp(steps), shape[position] // blocks).reshape((-1,) + (1,) * (len(shape) - 1 - position))
    return factor_of


def length_profile(amount, total, bound, skew):
    weights = [(1 << 20) // math.isqrt(rank ** skew) + 1 for rank in range(2, amount + 1)]
    spare, counts = total - bound - (amount - 1), [1] * (amount - 1)
    while spare > 0:
        candidates = [i for i in range(amount - 1) if counts[i] < bound]
        whole, remaining = sum([weights[i] for i in candidates]), spare
        for i in candidates:
            addition = min(bound - counts[i], max(1, remaining * weights[i] // whole), spare)
            counts[i] = counts[i] + addition
            spare = spare - addition
    return np.array([bound] + counts)


def uneven(stream_key, number_of, total, bound, slope):
    if number_of == 2:
        one = jax.random.randint(stream_key, (), max(1, total - bound), min(bound, total - 1) + 1)
        return jnp.stack([one, total - one])
    sizes = jnp.asarray(length_profile(number_of, total, bound, slope), jnp.int32)
    couples = (number_of - 1) // 2
    donor, taker = sizes[1:1 + 2 * couples:2], sizes[2:2 + 2 * couples:2]
    margin = jnp.minimum(donor - 1, bound - taker)
    moved = jax.random.randint(jax.random.fold_in(stream_key, 1), (couples,), 0, 1 << 20) % (margin + 1)
    sizes = sizes.at[1:1 + 2 * couples:2].set(donor - moved).at[2:2 + 2 * couples:2].set(taker + moved)
    return sizes[jax.random.permutation(jax.random.fold_in(stream_key, 2), number_of)]


def normal_values(key, shape, width, reach, shards=(), held_as=jnp.bfloat16):
    values = width * jax.random.normal(key, shape, jnp.float32)
    if shards:
        values = values * level_of(key, shape, shards, -0.22, 0.18)
    return jnp.clip(values, -reach, reach).astype(held_as)


def setup_inputs(seed: int = 0) -> dict:
    key_of = jax.random.split(jax.random.key(seed), 8)
    saved_inputs = normal_values(key_of[0], (LAYERS, MICRO, TOKENS, D), 1.0, 6.0, ((0, 4), (2, 8)))
    attn_weights = draw_attn_weights(jax.random.fold_in(key_of[7], 71), 0)
    grad_out = normal_values(key_of[2], (MICRO, TOKENS, D), 0.2, 1.1953125, ((1, 8),))
    segments = jax.vmap(lambda own: jnp.searchsorted(jnp.cumsum(uneven(own, SESS, ROWS, ROWS // 2, 0)), jnp.arange(ROWS), side="right"))(jax.random.split(key_of[3], MICRO * BLOCKS)).reshape((MICRO, BLOCKS, ROWS)).astype(jnp.int32)
    coords = normal_values(key_of[4], (3, MICRO, TOKENS), 1.0, 4.0, ((2, 8),), jnp.float32)
    embed_in = normal_values(key_of[5], (HID, 4), 1.0, 4.0, ((0, 32),))
    embed_out = normal_values(key_of[6], (HID, D), HID ** -0.5, 0.125, ((0, 32),))
    return {"saved_inputs": saved_inputs, "attn_weights": attn_weights, "grad_out": grad_out, "segments": segments, "coords": coords, "embed_in": embed_in, "embed_out": embed_out}


EPS = 1e-05

def gelu_value(pre):
    return 0.5 * pre * (1.0 + jax.scipy.special.erf(pre / jnp.sqrt(2.0)))

def gelu_slope(pre):
    return 0.5 * (1.0 + jax.scipy.special.erf(pre / jnp.sqrt(2.0))) + pre * jnp.exp(-0.5 * pre * pre) / jnp.sqrt(2.0 * jnp.pi)

def layer_backward(inputs, upstream, segment, weights):
    row_count = inputs.shape[0]
    attn_width = weights.shape[1] // 4
    head_count = attn_width // HEAD_DIM
    scaling = HEAD_DIM ** (-0.5)
    values = inputs.astype(jnp.float32)
    norm_scale = lax.rsqrt(lax.optimization_barrier(jnp.mean(values * values, axis=-1, keepdims=True)) + EPS)
    normed = (values * norm_scale).astype(jnp.bfloat16)
    projection = weights[:, :3 * attn_width]
    projected = jnp.dot(normed, projection, preferred_element_type=jnp.float32).astype(jnp.bfloat16)
    queries = projected[:, :attn_width].reshape(row_count, head_count, HEAD_DIM).astype(jnp.float32)
    key_rows = projected[:, attn_width:2 * attn_width].reshape(row_count, head_count, HEAD_DIM).astype(jnp.float32)
    value_rows = projected[:, 2 * attn_width:].reshape(row_count, head_count, HEAD_DIM).astype(jnp.float32)
    scores = jnp.einsum('qhd,khd->hqk', queries, key_rows) * scaling
    same_session = segment[:, None] == segment[None, :]
    scores = jnp.where(same_session[None], scores, -1e+30)
    row_peak = lax.optimization_barrier(jnp.max(scores, axis=-1, keepdims=True))
    exponent = jnp.exp(scores - row_peak)
    probabilities = exponent / lax.optimization_barrier(jnp.sum(exponent, axis=-1, keepdims=True))
    prob_rounded = probabilities.astype(jnp.bfloat16).astype(jnp.float32)
    attended = jnp.einsum('hqk,khd->qhd', prob_rounded, value_rows).astype(jnp.bfloat16).reshape(row_count, attn_width)
    grad_attended = jnp.dot(upstream, weights[:, 3 * attn_width:], preferred_element_type=jnp.float32).astype(jnp.bfloat16)
    grad_heads = grad_attended.reshape(row_count, head_count, HEAD_DIM).astype(jnp.float32)
    grad_prob = jnp.einsum('qhd,khd->hqk', grad_heads, value_rows)
    delta = lax.optimization_barrier(jnp.sum(probabilities * grad_prob, axis=-1, keepdims=True))
    grad_score = (probabilities * (grad_prob - delta) * scaling).astype(jnp.bfloat16).astype(jnp.float32)
    grad_query = jnp.einsum('hqk,khd->qhd', grad_score, key_rows)
    grad_key = jnp.einsum('hqk,qhd->khd', grad_score, queries)
    grad_value = jnp.einsum('hqk,qhd->khd', prob_rounded, grad_heads)
    grad_qkv = jnp.concatenate([grad_query.reshape(row_count, attn_width), grad_key.reshape(row_count, attn_width), grad_value.reshape(row_count, attn_width)], axis=1).astype(jnp.bfloat16)
    grad_normed = lax.dot_general(grad_qkv, projection, (((1,), (1,)), ((), ())), preferred_element_type=jnp.float32)
    grad_inputs = upstream.astype(jnp.float32) + norm_scale * grad_normed - values * norm_scale ** 3 * lax.optimization_barrier(jnp.mean(values * grad_normed, axis=-1, keepdims=True))
    return (grad_inputs.astype(jnp.bfloat16), normed, grad_qkv, attended)

def regroup(array):
    return array.reshape(MICRO, N_FSDP, ROWS, array.shape[-1]).transpose(1, 0, 2, 3).reshape(N_FSDP, MICRO * ROWS, array.shape[-1])

def weight_grad(normed, grad_qkv, upstream, attended):

    def accumulate(total, block):
        block_normed, block_qkv, block_up, block_att = block
        first = jnp.dot(block_normed.T, block_qkv, preferred_element_type=jnp.float32)
        second = jnp.dot(block_up.T, block_att, preferred_element_type=jnp.float32)
        partial_sum = lax.optimization_barrier(jnp.concatenate([first, second], axis=1).astype(jnp.bfloat16)).astype(jnp.float32)
        return (total + partial_sum, None)
    start = jnp.zeros((D, 4 * AW), jnp.float32)
    total, _ = lax.scan(accumulate, start, (regroup(normed), regroup(grad_qkv), regroup(upstream), regroup(attended)))
    return total

def reference(saved_inputs, attn_weights, grad_out, segments, coords, embed_in, embed_out):
    item_count = MICRO * N_FSDP
    segment_rows = segments.reshape(item_count, ROWS)
    upstream = grad_out.reshape(item_count, ROWS, D)
    layer_grads = []
    for layer in range(LAYERS - 1, -1, -1):
        inputs = saved_inputs[layer].reshape(item_count, ROWS, D)
        grad_inputs, normed, grad_qkv, attended = jax.vmap(layer_backward, in_axes=(0, 0, 0, None))(inputs, upstream, segment_rows, attn_weights[layer])
        layer_grads.append(weight_grad(normed.reshape(item_count * ROWS, D), grad_qkv.reshape(item_count * ROWS, 3 * AW), upstream.reshape(item_count * ROWS, D), attended.reshape(item_count * ROWS, AW)))
        upstream = grad_inputs
    attn_grad = jnp.stack(layer_grads[::-1])
    input_grad = upstream.reshape(MICRO, N_FSDP * ROWS, D)
    augmented = jnp.concatenate([coords, jnp.ones((1, MICRO, N_FSDP * ROWS), jnp.float32)], axis=0)
    aug_blocks = augmented.reshape(4, MICRO, N_FSDP, ROWS).transpose(2, 0, 1, 3).reshape(N_FSDP, 4, MICRO * ROWS)
    grad_blocks = regroup(input_grad.reshape(MICRO * N_FSDP * ROWS, D))
    embed_in_f = embed_in.astype(jnp.float32)

    def accumulate(totals, block):
        aug_rows, grad_rows = block
        pre = jnp.dot(embed_in_f, aug_rows, precision=lax.Precision.HIGHEST)
        hidden = gelu_value(pre).astype(jnp.bfloat16)
        term_out = jnp.dot(hidden, grad_rows, preferred_element_type=jnp.float32)
        grad_hidden = lax.dot_general(embed_out, grad_rows, (((1,), (1,)), ((), ())), preferred_element_type=jnp.float32)
        grad_pre = grad_hidden * gelu_slope(pre)
        term_in = lax.dot_general(grad_pre, aug_rows, (((1,), (1,)), ((), ())), precision=lax.Precision.HIGHEST)
        term_out = lax.optimization_barrier(term_out.astype(jnp.bfloat16)).astype(jnp.float32)
        term_in = lax.optimization_barrier(term_in.astype(jnp.bfloat16)).astype(jnp.float32)
        return ((totals[0] + term_out, totals[1] + term_in), None)
    start = (jnp.zeros((HID, D), jnp.float32), jnp.zeros((HID, 4), jnp.float32))
    totals, _ = lax.scan(accumulate, start, (aug_blocks, grad_blocks))
    return (attn_grad, input_grad, totals[0], totals[1])
```

```python
import functools

import jax
import jax.numpy as jnp
from jax import lax
from jax.experimental import pallas as pl
from jax.experimental.pallas import tpu as pltpu
from jax.sharding import PartitionSpec as P

HEAD_DIM = 64
PAIR = 2 * HEAD_DIM
EPS = 1e-05
CHUNKS = 4
VMEM_LIMIT = 40 * 1024 * 1024


def gelu_value(pre):
    return 0.5 * pre * (1.0 + jax.scipy.special.erf(pre / jnp.sqrt(2.0)))


def gelu_slope(pre):
    return 0.5 * (1.0 + jax.scipy.special.erf(pre / jnp.sqrt(2.0))) + pre * jnp.exp(
        -0.5 * pre * pre
    ) / jnp.sqrt(2.0 * jnp.pi)


def dot_nt(left, right):
    return lax.dot_general(
        left, right, (((1,), (1,)), ((), ())), preferred_element_type=jnp.float32
    )


def dot_tn(left, right):
    return lax.dot_general(
        left, right, (((0,), (0,)), ((), ())), preferred_element_type=jnp.float32
    )


def dot_nn(left, right):
    return jnp.dot(left, right, preferred_element_type=jnp.float32)


def half_masks(rows):
    low = lax.broadcasted_iota(jnp.int32, (rows, PAIR), 1) < HEAD_DIM
    return low


def forward_kernel(attn_width, qkv_ref, row_id_ref, col_id_ref, prob_ref, att_ref):
    rows = qkv_ref.shape[0]
    same = row_id_ref[...] == col_id_ref[...]
    low = half_masks(rows)
    zero = jnp.zeros((rows, PAIR), jnp.bfloat16)
    for pair in range(attn_width // PAIR):
        at = pair * PAIR
        query = qkv_ref[:, at : at + PAIR]
        key = qkv_ref[:, attn_width + at : attn_width + at + PAIR]
        value = qkv_ref[:, 2 * attn_width + at : 2 * attn_width + at + PAIR]
        parts = []
        for half in range(2):
            mine = low if half == 0 else jnp.logical_not(low)
            scores = dot_nt(jnp.where(mine, key, zero), query) * (HEAD_DIM**-0.5)
            scores = jnp.where(same, scores, -1e30)
            exponent = jnp.exp(scores - jnp.max(scores, axis=0, keepdims=True))
            prob = exponent / jnp.sum(exponent, axis=0, keepdims=True)
            prob_ref[2 * pair + half] = prob
            parts.append(dot_tn(prob.astype(jnp.bfloat16), value))
        att_ref[:, at : at + PAIR] = jnp.where(low, parts[0], parts[1]).astype(jnp.bfloat16)


def backward_kernel(attn_width, qkv_ref, up_ref, prob_ref, out_ref, sum_ref):
    rows = qkv_ref.shape[0]
    low = half_masks(rows)
    zero = jnp.zeros((rows, PAIR), jnp.bfloat16)
    total = jnp.zeros((rows, PAIR), jnp.float32)
    for pair in range(attn_width // PAIR):
        at = pair * PAIR
        query = qkv_ref[:, at : at + PAIR]
        key = qkv_ref[:, attn_width + at : attn_width + at + PAIR]
        value = qkv_ref[:, 2 * attn_width + at : 2 * attn_width + at + PAIR]
        up = up_ref[:, at : at + PAIR]
        parts = []
        for half in range(2):
            mine = low if half == 0 else jnp.logical_not(low)
            prob = prob_ref[2 * pair + half]
            grad_prob = dot_nt(jnp.where(mine, value, zero), up)
            delta = jnp.sum(prob * grad_prob, axis=0, keepdims=True)
            grad_score = (prob * (grad_prob - delta) * (HEAD_DIM**-0.5)).astype(jnp.bfloat16)
            parts.append(
                (
                    dot_tn(grad_score, key),
                    dot_nn(grad_score, query),
                    dot_nn(prob.astype(jnp.bfloat16), up),
                )
            )
        for place, own in enumerate((query, key, value)):
            grad = jnp.where(low, parts[0][place], parts[1][place]).astype(jnp.bfloat16)
            left = place * attn_width + at
            out_ref[:, left : left + PAIR] = grad
            total = total + own.astype(jnp.float32) * grad.astype(jnp.float32)
    sum_ref[...] = jnp.sum(total, axis=1, keepdims=True)


def whole_vmem(count):
    return [pl.BlockSpec(memory_space=pltpu.VMEM)] * count


def attention_forward(qkv, row_id):
    rows, attn_width = qkv.shape[0], qkv.shape[1] // 3
    heads = attn_width // HEAD_DIM
    return pl.pallas_call(
        functools.partial(forward_kernel, attn_width),
        out_shape=(
            jax.ShapeDtypeStruct((heads, rows, rows), jnp.float32),
            jax.ShapeDtypeStruct((rows, attn_width), jnp.bfloat16),
        ),
        in_specs=whole_vmem(3),
        out_specs=tuple(whole_vmem(2)),
        compiler_params=pltpu.CompilerParams(vmem_limit_bytes=VMEM_LIMIT),
        cost_estimate=pl.CostEstimate(
            flops=4 * rows * rows * attn_width,
            bytes_accessed=8 * rows * attn_width + 4 * heads * rows * rows,
            transcendentals=heads * rows * rows,
        ),
        name="attention_forward",
    )(qkv, row_id.reshape(rows, 1), row_id.reshape(1, rows))


def attention_backward(qkv, up, prob):
    rows, attn_width = qkv.shape[0], qkv.shape[1] // 3
    heads = attn_width // HEAD_DIM
    return pl.pallas_call(
        functools.partial(backward_kernel, attn_width),
        out_shape=(
            jax.ShapeDtypeStruct((rows, 3 * attn_width), jnp.bfloat16),
            jax.ShapeDtypeStruct((rows, 1), jnp.float32),
        ),
        in_specs=whole_vmem(3),
        out_specs=tuple(whole_vmem(2)),
        compiler_params=pltpu.CompilerParams(vmem_limit_bytes=VMEM_LIMIT),
        cost_estimate=pl.CostEstimate(
            flops=8 * rows * rows * attn_width,
            bytes_accessed=14 * rows * attn_width + 4 * heads * rows * rows,
            transcendentals=0,
        ),
        name="attention_backward",
    )(qkv, up, prob)


def on_device(saved_inputs, attn_weights, grad_out, segments, coords, embed_in, embed_out):
    section_count = lax.axis_size("section")
    section_index = lax.axis_index("section")
    micro_count, row_count, width = saved_inputs.shape[1:]
    attn_width = attn_weights.shape[2] // 4
    rows = micro_count * row_count
    weights = lax.all_gather(attn_weights[0], "fsdp", axis=0, tiled=True)
    projection, output_weights = weights[:, : 3 * attn_width], weights[:, 3 * attn_width :]
    places = lax.all_gather(coords.reshape(3, rows), "fsdp", axis=1, tiled=True)
    augmented = jnp.concatenate([places, jnp.ones_like(places[:1])], axis=0)
    pre = jnp.dot(embed_in.astype(jnp.float32), augmented, precision=lax.Precision.HIGHEST)
    hidden, slope = gelu_value(pre).astype(jnp.bfloat16), gelu_slope(pre)

    values = saved_inputs[0].reshape(rows, width).astype(jnp.float32)
    norm_scale = lax.rsqrt(jnp.mean(values * values, axis=-1, keepdims=True) + EPS)
    normed = (values * norm_scale).astype(jnp.bfloat16)
    normed_columns = lax.all_to_all(normed, "fsdp", split_axis=1, concat_axis=0, tiled=True)
    micro = lax.broadcasted_iota(jnp.int32, (micro_count, row_count), 0)
    row_id = (segments[:, 0, :] + micro * 1024).reshape(rows)

    qkv = dot_nn(normed, projection).astype(jnp.bfloat16)
    prob, attended = attention_forward(qkv, row_id)
    attended_all = lax.all_gather(attended, "fsdp", axis=0, tiled=True)

    chunk = width // CHUNKS
    top = grad_out.reshape(rows, width)
    upstream = [top[:, c * chunk : (c + 1) * chunk] for c in range(CHUNKS)]
    is_top = section_index == section_count - 1
    down = [(i, i - 1) for i in range(1, section_count)]
    for step in range(section_count):
        if step > 0:
            upstream = [
                jnp.where(is_top, top[:, c * chunk : (c + 1) * chunk], received[c])
                for c in range(CHUNKS)
            ]
        grad_attended = sum(
            dot_nn(upstream[c], output_weights[c * chunk : (c + 1) * chunk])
            for c in range(CHUNKS)
        ).astype(jnp.bfloat16)
        grad_qkv, row_sum = attention_backward(qkv, grad_attended, prob)
        shrink = norm_scale * norm_scale * row_sum / width
        received, grad_inputs = [], []
        for c in range(CHUNKS):
            cut = slice(c * chunk, (c + 1) * chunk)
            fresh = (
                upstream[c].astype(jnp.float32)
                + norm_scale * dot_nt(grad_qkv, projection[cut])
                - values[:, cut] * shrink
            ).astype(jnp.bfloat16)
            grad_inputs.append(fresh)
            if step < section_count - 1:
                received.append(lax.ppermute(fresh, "section", down))

    upstream_columns = lax.all_to_all(
        jnp.concatenate(upstream, axis=1), "fsdp", split_axis=1, concat_axis=0, tiled=True
    )
    qkv_all = lax.all_gather(grad_qkv, "fsdp", axis=0, tiled=True)
    attn_grad = jnp.concatenate(
        [dot_tn(normed_columns, qkv_all), dot_tn(upstream_columns, attended_all)], axis=1
    )
    lowest = jnp.concatenate(grad_inputs, axis=1)
    lowest = jnp.where(section_index == 0, lowest, jnp.zeros_like(lowest))
    input_grad = lax.psum(lowest, "section")
    input_all = lax.all_gather(input_grad, "fsdp", axis=0, tiled=True)
    embed_out_grad = dot_nn(hidden, input_all)
    grad_pre = dot_nt(embed_out, input_all) * slope
    embed_in_grad = lax.dot_general(
        grad_pre, augmented, (((1,), (1,)), ((), ())), precision=lax.Precision.HIGHEST
    )
    return (
        attn_grad[None],
        input_grad.reshape(micro_count, row_count, width),
        embed_out_grad,
        embed_in_grad,
    )


def solution(mesh):
    placed = (
        P("section", None, "fsdp", None),
        P("section", "fsdp", None),
        P(None, "fsdp", None),
        P(None, "fsdp", None),
        P(None, None, "fsdp"),
        P(("section", "fsdp"), None),
        P(("section", "fsdp"), None),
    )
    return jax.shard_map(
        on_device,
        mesh=mesh,
        in_specs=placed,
        out_specs=(
            P("section", "fsdp", None),
            P(None, "fsdp", None),
            P(("section", "fsdp"), None),
            P(("section", "fsdp"), None),
        ),
        check_vma=False,
    )
```

```python
import functools

import jax
import jax.numpy as jnp
from jax import lax
from jax.experimental import pallas as pl
from jax.experimental.pallas import tpu as pltpu
from jax.sharding import PartitionSpec as P

HEAD_DIM = 64
PAIR = 2 * HEAD_DIM
EPS = 1e-05
CHUNKS = 4
MESH = pl.DeviceIdType.MESH
VMEM_LIMIT = 40 * 1024 * 1024


def gelu_value(pre):
    return 0.5 * pre * (1.0 + jax.scipy.special.erf(pre / jnp.sqrt(2.0)))


def gelu_slope(pre):
    return 0.5 * (1.0 + jax.scipy.special.erf(pre / jnp.sqrt(2.0))) + pre * jnp.exp(
        -0.5 * pre * pre
    ) / jnp.sqrt(2.0 * jnp.pi)


def dot_nt(left, right):
    return lax.dot_general(
        left, right, (((1,), (1,)), ((), ())), preferred_element_type=jnp.float32
    )


def dot_tn(left, right):
    return lax.dot_general(
        left, right, (((0,), (0,)), ((), ())), preferred_element_type=jnp.float32
    )


def dot_nn(left, right):
    return jnp.dot(left, right, preferred_element_type=jnp.float32)


def half_masks(rows):
    low = lax.broadcasted_iota(jnp.int32, (rows, PAIR), 1) < HEAD_DIM
    return low


def forward_kernel(attn_width, qkv_ref, row_id_ref, col_id_ref, prob_ref, att_ref):
    rows = qkv_ref.shape[0]
    same = row_id_ref[...] == col_id_ref[...]
    low = half_masks(rows)
    zero = jnp.zeros((rows, PAIR), jnp.bfloat16)
    for pair in range(attn_width // PAIR):
        at = pair * PAIR
        query = qkv_ref[:, at : at + PAIR]
        key = qkv_ref[:, attn_width + at : attn_width + at + PAIR]
        value = qkv_ref[:, 2 * attn_width + at : 2 * attn_width + at + PAIR]
        parts = []
        for half in range(2):
            mine = low if half == 0 else jnp.logical_not(low)
            scores = dot_nt(jnp.where(mine, key, zero), query) * (HEAD_DIM**-0.5)
            scores = jnp.where(same, scores, -1e30)
            exponent = jnp.exp(scores - jnp.max(scores, axis=0, keepdims=True))
            prob = exponent / jnp.sum(exponent, axis=0, keepdims=True)
            prob_ref[2 * pair + half] = prob
            parts.append(dot_tn(prob.astype(jnp.bfloat16), value))
        att_ref[:, at : at + PAIR] = jnp.where(low, parts[0], parts[1]).astype(jnp.bfloat16)


def backward_kernel(attn_width, qkv_ref, up_ref, prob_ref, out_ref, sum_ref):
    rows = qkv_ref.shape[0]
    low = half_masks(rows)
    zero = jnp.zeros((rows, PAIR), jnp.bfloat16)
    total = jnp.zeros((rows, PAIR), jnp.float32)
    for pair in range(attn_width // PAIR):
        at = pair * PAIR
        query = qkv_ref[:, at : at + PAIR]
        key = qkv_ref[:, attn_width + at : attn_width + at + PAIR]
        value = qkv_ref[:, 2 * attn_width + at : 2 * attn_width + at + PAIR]
        up = up_ref[:, at : at + PAIR]
        parts = []
        for half in range(2):
            mine = low if half == 0 else jnp.logical_not(low)
            prob = prob_ref[2 * pair + half]
            grad_prob = dot_nt(jnp.where(mine, value, zero), up)
            delta = jnp.sum(prob * grad_prob, axis=0, keepdims=True)
            grad_score = (prob * (grad_prob - delta) * (HEAD_DIM**-0.5)).astype(jnp.bfloat16)
            parts.append(
                (
                    dot_tn(grad_score, key),
                    dot_nn(grad_score, query),
                    dot_nn(prob.astype(jnp.bfloat16), up),
                )
            )
        for place, own in enumerate((query, key, value)):
            grad = jnp.where(low, parts[0][place], parts[1][place]).astype(jnp.bfloat16)
            left = place * attn_width + at
            out_ref[:, left : left + PAIR] = grad
            total = total + own.astype(jnp.float32) * grad.astype(jnp.float32)
    sum_ref[...] = jnp.sum(total, axis=1, keepdims=True)


def whole_vmem(count):
    return [pl.BlockSpec(memory_space=pltpu.VMEM)] * count


def attention_forward(qkv, row_id):
    rows, attn_width = qkv.shape[0], qkv.shape[1] // 3
    heads = attn_width // HEAD_DIM
    return pl.pallas_call(
        functools.partial(forward_kernel, attn_width),
        out_shape=(
            jax.ShapeDtypeStruct((heads, rows, rows), jnp.float32),
            jax.ShapeDtypeStruct((rows, attn_width), jnp.bfloat16),
        ),
        in_specs=whole_vmem(3),
        out_specs=tuple(whole_vmem(2)),
        compiler_params=pltpu.CompilerParams(vmem_limit_bytes=VMEM_LIMIT),
        cost_estimate=pl.CostEstimate(
            flops=4 * rows * rows * attn_width,
            bytes_accessed=8 * rows * attn_width + 4 * heads * rows * rows,
            transcendentals=heads * rows * rows,
        ),
        name="attention_forward",
    )(qkv, row_id.reshape(rows, 1), row_id.reshape(1, rows))


def attention_backward(qkv, up, prob):
    rows, attn_width = qkv.shape[0], qkv.shape[1] // 3
    heads = attn_width // HEAD_DIM
    return pl.pallas_call(
        functools.partial(backward_kernel, attn_width),
        out_shape=(
            jax.ShapeDtypeStruct((rows, 3 * attn_width), jnp.bfloat16),
            jax.ShapeDtypeStruct((rows, 1), jnp.float32),
        ),
        in_specs=whole_vmem(3),
        out_specs=tuple(whole_vmem(2)),
        compiler_params=pltpu.CompilerParams(vmem_limit_bytes=VMEM_LIMIT),
        cost_estimate=pl.CostEstimate(
            flops=8 * rows * rows * attn_width,
            bytes_accessed=14 * rows * attn_width + 4 * heads * rows * rows,
            transcendentals=0,
        ),
        name="attention_backward",
    )(qkv, up, prob)


def gather_plan(shard_ref, out_ref, send_sems, recv_sems, local_sem):
    section, me = lax.axis_index("section"), lax.axis_index("fsdp")
    core, first, second = me % 2, (me // 2) % 2, me // 4
    rows = shard_ref.shape[0]
    half_rows = rows // 2

    def device(bits):
        other_core = core + (1 - 2 * core) * (bits % 2)
        other_first = first + (1 - 2 * first) * (bits // 2 % 2)
        other_second = second + (1 - 2 * second) * (bits // 4)
        return other_second * 4 + other_first * 2 + other_core

    def place(bits, half):
        start = pl.multiple_of(device(bits) * rows + half * half_rows, half_rows)
        return out_ref.at[pl.ds(start, half_rows)]

    def copy(bits, half, to):
        source = shard_ref.at[pl.ds(half * half_rows, half_rows)] if bits == 0 else place(bits, half)
        arrives = bits + to
        return pltpu.make_async_remote_copy(
            src_ref=source,
            dst_ref=place(bits, half),
            send_sem=send_sems.at[arrives * 2 + half],
            recv_sem=recv_sems.at[arrives * 2 + half],
            device_id=(section, device(to)),
            device_id_type=MESH,
        )

    def arrived(bits, half):
        pltpu.make_async_remote_copy(
            src_ref=place(bits, half),
            dst_ref=place(bits, half),
            send_sem=send_sems.at[bits * 2 + half],
            recv_sem=recv_sems.at[bits * 2 + half],
            device_id=(section, device(1)),
            device_id_type=MESH,
        ).wait_recv()

    started = []

    def send(bits, half, to):
        each = copy(bits, half, to)
        each.start()
        started.append(each)

    own = pltpu.make_async_copy(
        shard_ref, out_ref.at[pl.ds(pl.multiple_of(me * rows, rows), rows)], local_sem
    )

    def begin():
        send(0, 0, 2)
        send(0, 1, 4)
        send(0, 0, 4)
        send(0, 1, 2)
        send(0, 0, 1)
        send(0, 1, 1)
        own.start()

    def relay():
        arrived(2, 0)
        send(2, 0, 4)
        send(2, 0, 1)
        arrived(4, 1)
        send(4, 1, 2)
        send(4, 1, 1)

    def hand_over():
        for bits, half in ((4, 0), (2, 1), (6, 0), (6, 1)):
            arrived(bits, half)
            send(bits, half, 1)

    def finish():
        for bits in (1, 3, 5, 7):
            arrived(bits, 0)
            arrived(bits, 1)
        for each in started:
            each.wait_send()
        own.wait()

    return begin, relay, hand_over, finish


def greet(along_section):
    section, me = lax.axis_index("section"), lax.axis_index("fsdp")
    core, first, second = me % 2, (me // 2) % 2, me // 4
    barrier = pltpu.get_barrier_semaphore()
    for other in (me + 1 - 2 * core, me + 2 * (1 - 2 * first), me + 4 * (1 - 2 * second)):
        pl.semaphore_signal(barrier, inc=1, device_id=(section, other), device_id_type=MESH)
    if not along_section:
        pl.semaphore_wait(barrier, 3)
        return
    last = lax.axis_size("section") - 1

    @pl.when(section > 0)
    def _():
        pl.semaphore_signal(barrier, inc=1, device_id=(section - 1, me), device_id_type=MESH)

    @pl.when(section < last)
    def _():
        pl.semaphore_signal(barrier, inc=1, device_id=(section + 1, me), device_id_type=MESH)

    @pl.when(jnp.logical_or(section == 0, section == last))
    def _():
        pl.semaphore_wait(barrier, 4)

    @pl.when(jnp.logical_and(section > 0, section < last))
    def _():
        pl.semaphore_wait(barrier, 5)


def gather_kernel(count, *refs):
    shards, outs, (send_sems, recv_sems, local_sems) = refs[:count], refs[count : 2 * count], refs[2 * count :]
    greet(False)
    plans = [
        gather_plan(shards[i], outs[i], send_sems.at[i], recv_sems.at[i], local_sems.at[i])
        for i in range(count)
    ]
    for stage in range(4):
        for plan in plans:
            plan[stage]()


def spread_kernel(
    qkv_ref, low_ref, qkv_all_ref, own_ref, all_ref, send_sems, recv_sems, local_sems, up_send, up_recv
):
    section, me = lax.axis_index("section"), lax.axis_index("fsdp")
    last = lax.axis_size("section") - 1
    chunk = low_ref.shape[0] // CHUNKS
    greet(True)
    first = gather_plan(qkv_ref, qkv_all_ref, send_sems.at[0], recv_sems.at[0], local_sems.at[0])
    second = gather_plan(own_ref, all_ref, send_sems.at[1], recv_sems.at[1], local_sems.at[1])
    keep = pltpu.make_async_copy(low_ref, own_ref, local_sems.at[2])

    def upward(source, c):
        cut = pl.ds(c * chunk, chunk)
        return pltpu.make_async_remote_copy(
            src_ref=source.at[cut],
            dst_ref=own_ref.at[cut],
            send_sem=up_send.at[c],
            recv_sem=up_recv.at[c],
            device_id=(jnp.minimum(section + 1, last), me),
            device_id_type=MESH,
        )

    @pl.when(section == 0)
    def _():
        for c in range(CHUNKS):
            upward(low_ref, c).start()
        keep.start()

    first[0]()

    @pl.when(section == 0)
    def _():
        keep.wait()

    for c in range(CHUNKS):

        @pl.when(section > 0)
        def _():
            upward(own_ref, c).wait_recv()

        @pl.when(jnp.logical_and(section > 0, section < last))
        def _():
            upward(own_ref, c).start()

    first[1]()
    second[0]()
    first[2]()
    second[1]()
    second[2]()
    first[3]()
    second[3]()

    @pl.when(section < last)
    def _():
        for c in range(CHUNKS):
            upward(own_ref, c).wait_send()


def anywhere(count):
    return [pl.BlockSpec(memory_space=pl.ANY)] * count


def whole_of(shard):
    devices = lax.axis_size("fsdp")
    return jax.ShapeDtypeStruct((devices * shard.shape[0],) + shard.shape[1:], shard.dtype)


def gather_all(*shards):
    if lax.axis_size("fsdp") != 8:
        return tuple(lax.all_gather(shard, "fsdp", axis=0, tiled=True) for shard in shards)
    count = len(shards)
    return pl.pallas_call(
        functools.partial(gather_kernel, count),
        out_shape=tuple(whole_of(shard) for shard in shards),
        in_specs=anywhere(count),
        out_specs=tuple(anywhere(count)),
        scratch_shapes=[
            pltpu.SemaphoreType.DMA((count, 16)),
            pltpu.SemaphoreType.DMA((count, 16)),
            pltpu.SemaphoreType.DMA((count,)),
        ],
        compiler_params=pltpu.CompilerParams(collective_id=0, has_side_effects=True),
        name="gather_weights",
    )(*shards)


def gather_and_spread(grad_qkv, lowest):
    if lax.axis_size("fsdp") != 8 or lax.axis_size("section") < 2:
        lowest = jnp.where(lax.axis_index("section") == 0, lowest, jnp.zeros_like(lowest))
        input_grad = lax.psum(lowest, "section")
        return (
            lax.all_gather(grad_qkv, "fsdp", axis=0, tiled=True),
            input_grad,
            lax.all_gather(input_grad, "fsdp", axis=0, tiled=True),
        )
    return pl.pallas_call(
        spread_kernel,
        out_shape=(
            whole_of(grad_qkv),
            jax.ShapeDtypeStruct(lowest.shape, lowest.dtype),
            whole_of(lowest),
        ),
        in_specs=anywhere(2),
        out_specs=tuple(anywhere(3)),
        scratch_shapes=[
            pltpu.SemaphoreType.DMA((2, 16)),
            pltpu.SemaphoreType.DMA((2, 16)),
            pltpu.SemaphoreType.DMA((3,)),
            pltpu.SemaphoreType.DMA((CHUNKS,)),
            pltpu.SemaphoreType.DMA((CHUNKS,)),
        ],
        compiler_params=pltpu.CompilerParams(collective_id=1, has_side_effects=True),
        name="gather_gradients",
    )(grad_qkv, lowest)


def on_device(saved_inputs, attn_weights, grad_out, segments, coords, embed_in, embed_out):
    section_count = lax.axis_size("section")
    section_index = lax.axis_index("section")
    micro_count, row_count, width = saved_inputs.shape[1:]
    attn_width = attn_weights.shape[2] // 4
    rows = micro_count * row_count
    placed = jnp.pad(coords.reshape(3, rows), ((0, 13), (0, -rows % 128)))
    weights, places = gather_all(attn_weights[0], placed)
    projection, output_weights = weights[:, : 3 * attn_width], weights[:, 3 * attn_width :]
    places = places.reshape(-1, 16, placed.shape[1])[:, :3, :rows]
    places = places.transpose(1, 0, 2).reshape(3, -1)
    augmented = jnp.concatenate([places, jnp.ones_like(places[:1])], axis=0)
    pre = jnp.dot(embed_in.astype(jnp.float32), augmented, precision=lax.Precision.HIGHEST)
    hidden, slope = gelu_value(pre).astype(jnp.bfloat16), gelu_slope(pre)

    values = saved_inputs[0].reshape(rows, width).astype(jnp.float32)
    norm_scale = lax.rsqrt(jnp.mean(values * values, axis=-1, keepdims=True) + EPS)
    normed = (values * norm_scale).astype(jnp.bfloat16)
    normed_columns = lax.all_to_all(normed, "fsdp", split_axis=1, concat_axis=0, tiled=True)
    micro = lax.broadcasted_iota(jnp.int32, (micro_count, row_count), 0)
    row_id = (segments[:, 0, :] + micro * 1024).reshape(rows)

    qkv = dot_nn(normed, projection).astype(jnp.bfloat16)
    prob, attended = attention_forward(qkv, row_id)
    attended_all = lax.all_gather(attended, "fsdp", axis=0, tiled=True)

    chunk = width // CHUNKS
    top = grad_out.reshape(rows, width)
    upstream = [top[:, c * chunk : (c + 1) * chunk] for c in range(CHUNKS)]
    is_top = section_index == section_count - 1
    down = [(i, i - 1) for i in range(1, section_count)]
    for step in range(section_count):
        if step > 0:
            upstream = [
                jnp.where(is_top, top[:, c * chunk : (c + 1) * chunk], received[c])
                for c in range(CHUNKS)
            ]
        grad_attended = sum(
            dot_nn(upstream[c], output_weights[c * chunk : (c + 1) * chunk])
            for c in range(CHUNKS)
        ).astype(jnp.bfloat16)
        grad_qkv, row_sum = attention_backward(qkv, grad_attended, prob)
        shrink = norm_scale * norm_scale * row_sum / width
        received, grad_inputs = [], []
        for c in range(CHUNKS):
            cut = slice(c * chunk, (c + 1) * chunk)
            fresh = (
                upstream[c].astype(jnp.float32)
                + norm_scale * dot_nt(grad_qkv, projection[cut])
                - values[:, cut] * shrink
            ).astype(jnp.bfloat16)
            grad_inputs.append(fresh)
            if step < section_count - 1:
                received.append(lax.ppermute(fresh, "section", down))

    upstream_columns = lax.all_to_all(
        jnp.concatenate(upstream, axis=1), "fsdp", split_axis=1, concat_axis=0, tiled=True
    )
    lowest = jnp.concatenate(grad_inputs, axis=1)
    qkv_all, input_grad, input_all = gather_and_spread(grad_qkv, lowest)
    attn_grad = jnp.concatenate(
        [dot_tn(normed_columns, qkv_all), dot_tn(upstream_columns, attended_all)], axis=1
    )
    embed_out_grad = dot_nn(hidden, input_all)
    grad_pre = dot_nt(embed_out, input_all) * slope
    embed_in_grad = lax.dot_general(
        grad_pre, augmented, (((1,), (1,)), ((), ())), precision=lax.Precision.HIGHEST
    )
    return (
        attn_grad[None],
        input_grad.reshape(micro_count, row_count, width),
        embed_out_grad,
        embed_in_grad,
    )


def solution(mesh):
    placed = (
        P("section", None, "fsdp", None),
        P("section", "fsdp", None),
        P(None, "fsdp", None),
        P(None, "fsdp", None),
        P(None, None, "fsdp"),
        P(("section", "fsdp"), None),
        P(("section", "fsdp"), None),
    )
    return jax.shard_map(
        on_device,
        mesh=mesh,
        in_specs=placed,
        out_specs=(
            P("section", "fsdp", None),
            P(None, "fsdp", None),
            P(("section", "fsdp"), None),
            P(("section", "fsdp"), None),
        ),
        check_vma=False,
    )
```

```python
import functools

import jax
import jax.numpy as jnp
from jax import lax
from jax.experimental import pallas as pl
from jax.experimental.pallas import tpu as pltpu
from jax.sharding import PartitionSpec as P

HEAD_DIM = 64
PAIR = 2 * HEAD_DIM
EPS = 1e-05
CHUNKS = 4
BLOCK = 512
MESH = pl.DeviceIdType.MESH
VMEM_LIMIT = 40 * 1024 * 1024


def gelu_value(pre):
    return 0.5 * pre * (1.0 + jax.scipy.special.erf(pre / jnp.sqrt(2.0)))


def gelu_slope(pre):
    return 0.5 * (1.0 + jax.scipy.special.erf(pre / jnp.sqrt(2.0))) + pre * jnp.exp(
        -0.5 * pre * pre
    ) / jnp.sqrt(2.0 * jnp.pi)


def dot_nt(left, right):
    return lax.dot_general(
        left, right, (((1,), (1,)), ((), ())), preferred_element_type=jnp.float32
    )


def dot_tn(left, right):
    return lax.dot_general(
        left, right, (((0,), (0,)), ((), ())), preferred_element_type=jnp.float32
    )


def dot_nn(left, right):
    return jnp.dot(left, right, preferred_element_type=jnp.float32)


def half_masks(rows):
    low = lax.broadcasted_iota(jnp.int32, (rows, PAIR), 1) < HEAD_DIM
    return low


def forward_kernel(attn_width, qkv_ref, row_id_ref, col_id_ref, prob_ref, att_ref):
    rows = qkv_ref.shape[0]
    same = row_id_ref[...] == col_id_ref[...]
    low = half_masks(rows)
    zero = jnp.zeros((rows, PAIR), jnp.bfloat16)
    for pair in range(attn_width // PAIR):
        at = pair * PAIR
        query = qkv_ref[:, at : at + PAIR]
        key = qkv_ref[:, attn_width + at : attn_width + at + PAIR]
        value = qkv_ref[:, 2 * attn_width + at : 2 * attn_width + at + PAIR]
        parts = []
        for half in range(2):
            mine = low if half == 0 else jnp.logical_not(low)
            scores = dot_nt(jnp.where(mine, key, zero), query) * (HEAD_DIM**-0.5)
            scores = jnp.where(same, scores, -1e30)
            exponent = jnp.exp(scores - jnp.max(scores, axis=0, keepdims=True))
            prob = exponent / jnp.sum(exponent, axis=0, keepdims=True)
            prob_ref[2 * pair + half] = prob
            parts.append(dot_tn(prob.astype(jnp.bfloat16), value))
        att_ref[:, at : at + PAIR] = jnp.where(low, parts[0], parts[1]).astype(jnp.bfloat16)


def backward_kernel(attn_width, qkv_ref, up_ref, prob_ref, out_ref, sum_ref):
    rows = qkv_ref.shape[0]
    low = half_masks(rows)
    zero = jnp.zeros((rows, PAIR), jnp.bfloat16)
    total = jnp.zeros((rows, PAIR), jnp.float32)
    for pair in range(attn_width // PAIR):
        at = pair * PAIR
        query = qkv_ref[:, at : at + PAIR]
        key = qkv_ref[:, attn_width + at : attn_width + at + PAIR]
        value = qkv_ref[:, 2 * attn_width + at : 2 * attn_width + at + PAIR]
        up = up_ref[:, at : at + PAIR]
        parts = []
        for half in range(2):
            mine = low if half == 0 else jnp.logical_not(low)
            prob = prob_ref[2 * pair + half]
            grad_prob = dot_nt(jnp.where(mine, value, zero), up)
            delta = jnp.sum(prob * grad_prob, axis=0, keepdims=True)
            grad_score = (prob * (grad_prob - delta) * (HEAD_DIM**-0.5)).astype(jnp.bfloat16)
            parts.append(
                (
                    dot_tn(grad_score, key),
                    dot_nn(grad_score, query),
                    dot_nn(prob.astype(jnp.bfloat16), up),
                )
            )
        for place, own in enumerate((query, key, value)):
            grad = jnp.where(low, parts[0][place], parts[1][place]).astype(jnp.bfloat16)
            left = place * attn_width + at
            out_ref[:, left : left + PAIR] = grad
            total = total + own.astype(jnp.float32) * grad.astype(jnp.float32)
    sum_ref[...] = jnp.sum(total, axis=1, keepdims=True)


def whole_vmem(count):
    return [pl.BlockSpec(memory_space=pltpu.VMEM)] * count


def attention_forward(qkv, row_id):
    rows, attn_width = qkv.shape[0], qkv.shape[1] // 3
    heads = attn_width // HEAD_DIM
    return pl.pallas_call(
        functools.partial(forward_kernel, attn_width),
        out_shape=(
            jax.ShapeDtypeStruct((heads, rows, rows), jnp.float32),
            jax.ShapeDtypeStruct((rows, attn_width), jnp.bfloat16),
        ),
        in_specs=whole_vmem(3),
        out_specs=tuple(whole_vmem(2)),
        compiler_params=pltpu.CompilerParams(vmem_limit_bytes=VMEM_LIMIT),
        cost_estimate=pl.CostEstimate(
            flops=4 * rows * rows * attn_width,
            bytes_accessed=8 * rows * attn_width + 4 * heads * rows * rows,
            transcendentals=heads * rows * rows,
        ),
        name="attention_forward",
    )(qkv, row_id.reshape(rows, 1), row_id.reshape(1, rows))


def attention_backward(qkv, up, prob):
    rows, attn_width = qkv.shape[0], qkv.shape[1] // 3
    heads = attn_width // HEAD_DIM
    return pl.pallas_call(
        functools.partial(backward_kernel, attn_width),
        out_shape=(
            jax.ShapeDtypeStruct((rows, 3 * attn_width), jnp.bfloat16),
            jax.ShapeDtypeStruct((rows, 1), jnp.float32),
        ),
        in_specs=whole_vmem(3),
        out_specs=tuple(whole_vmem(2)),
        compiler_params=pltpu.CompilerParams(vmem_limit_bytes=VMEM_LIMIT),
        cost_estimate=pl.CostEstimate(
            flops=8 * rows * rows * attn_width,
            bytes_accessed=14 * rows * attn_width + 4 * heads * rows * rows,
            transcendentals=0,
        ),
        name="attention_backward",
    )(qkv, up, prob)


def gather_plan(shard_ref, out_ref, send_sems, recv_sems, local_sem):
    section, me = lax.axis_index("section"), lax.axis_index("fsdp")
    core, first, second = me % 2, (me // 2) % 2, me // 4
    rows = shard_ref.shape[0]
    half_rows = rows // 2

    def device(bits):
        other_core = core + (1 - 2 * core) * (bits % 2)
        other_first = first + (1 - 2 * first) * (bits // 2 % 2)
        other_second = second + (1 - 2 * second) * (bits // 4)
        return other_second * 4 + other_first * 2 + other_core

    def place(bits, half):
        start = pl.multiple_of(device(bits) * rows + half * half_rows, half_rows)
        return out_ref.at[pl.ds(start, half_rows)]

    def copy(bits, half, to):
        source = shard_ref.at[pl.ds(half * half_rows, half_rows)] if bits == 0 else place(bits, half)
        arrives = bits + to
        return pltpu.make_async_remote_copy(
            src_ref=source,
            dst_ref=place(bits, half),
            send_sem=send_sems.at[arrives * 2 + half],
            recv_sem=recv_sems.at[arrives * 2 + half],
            device_id=(section, device(to)),
            device_id_type=MESH,
        )

    def arrived(bits, half):
        pltpu.make_async_remote_copy(
            src_ref=place(bits, half),
            dst_ref=place(bits, half),
            send_sem=send_sems.at[bits * 2 + half],
            recv_sem=recv_sems.at[bits * 2 + half],
            device_id=(section, device(1)),
            device_id_type=MESH,
        ).wait_recv()

    started = []

    def send(bits, half, to):
        each = copy(bits, half, to)
        each.start()
        started.append(each)

    own = pltpu.make_async_copy(
        shard_ref, out_ref.at[pl.ds(pl.multiple_of(me * rows, rows), rows)], local_sem
    )

    def begin():
        send(0, 0, 2)
        send(0, 1, 4)
        send(0, 0, 4)
        send(0, 1, 2)
        send(0, 0, 1)
        send(0, 1, 1)
        own.start()

    def relay():
        arrived(2, 0)
        send(2, 0, 4)
        send(2, 0, 1)
        arrived(4, 1)
        send(4, 1, 2)
        send(4, 1, 1)

    def hand_over():
        for bits, half in ((4, 0), (2, 1), (6, 0), (6, 1)):
            arrived(bits, half)
            send(bits, half, 1)

    def finish():
        for bits in (1, 3, 5, 7):
            arrived(bits, 0)
            arrived(bits, 1)
        for each in started:
            each.wait_send()
        own.wait()

    return begin, relay, hand_over, finish


def greet(along_section):
    section, me = lax.axis_index("section"), lax.axis_index("fsdp")
    core, first, second = me % 2, (me // 2) % 2, me // 4
    barrier = pltpu.get_barrier_semaphore()
    for other in (me + 1 - 2 * core, me + 2 * (1 - 2 * first), me + 4 * (1 - 2 * second)):
        pl.semaphore_signal(barrier, inc=1, device_id=(section, other), device_id_type=MESH)
    if not along_section:
        pl.semaphore_wait(barrier, 3)
        return
    last = lax.axis_size("section") - 1

    @pl.when(section > 0)
    def _():
        pl.semaphore_signal(barrier, inc=1, device_id=(section - 1, me), device_id_type=MESH)

    @pl.when(section < last)
    def _():
        pl.semaphore_signal(barrier, inc=1, device_id=(section + 1, me), device_id_type=MESH)

    @pl.when(jnp.logical_or(section == 0, section == last))
    def _():
        pl.semaphore_wait(barrier, 4)

    @pl.when(jnp.logical_and(section > 0, section < last))
    def _():
        pl.semaphore_wait(barrier, 5)


def gather_kernel(count, *refs):
    shards, outs, (send_sems, recv_sems, local_sems) = refs[:count], refs[count : 2 * count], refs[2 * count :]
    greet(False)
    plans = [
        gather_plan(shards[i], outs[i], send_sems.at[i], recv_sems.at[i], local_sems.at[i])
        for i in range(count)
    ]
    for stage in range(4):
        for plan in plans:
            plan[stage]()


def spread_kernel(
    qkv_ref, low_ref, qkv_all_ref, own_ref, all_ref, send_sems, recv_sems, local_sems, up_send, up_recv
):
    section, me = lax.axis_index("section"), lax.axis_index("fsdp")
    last = lax.axis_size("section") - 1
    chunk = low_ref.shape[0] // CHUNKS
    greet(True)
    first = gather_plan(qkv_ref, qkv_all_ref, send_sems.at[0], recv_sems.at[0], local_sems.at[0])
    second = gather_plan(own_ref, all_ref, send_sems.at[1], recv_sems.at[1], local_sems.at[1])
    keep = pltpu.make_async_copy(low_ref, own_ref, local_sems.at[2])

    def upward(source, c):
        cut = pl.ds(c * chunk, chunk)
        return pltpu.make_async_remote_copy(
            src_ref=source.at[cut],
            dst_ref=own_ref.at[cut],
            send_sem=up_send.at[c],
            recv_sem=up_recv.at[c],
            device_id=(jnp.minimum(section + 1, last), me),
            device_id_type=MESH,
        )

    @pl.when(section == 0)
    def _():
        for c in range(CHUNKS):
            upward(low_ref, c).start()
        keep.start()

    first[0]()

    @pl.when(section == 0)
    def _():
        keep.wait()

    for c in range(CHUNKS):

        @pl.when(section > 0)
        def _():
            upward(own_ref, c).wait_recv()

        @pl.when(jnp.logical_and(section > 0, section < last))
        def _():
            upward(own_ref, c).start()

    first[1]()
    second[0]()
    first[2]()
    second[1]()
    second[2]()
    first[3]()
    second[3]()

    @pl.when(section < last)
    def _():
        for c in range(CHUNKS):
            upward(own_ref, c).wait_send()


def anywhere(count):
    return [pl.BlockSpec(memory_space=pl.ANY)] * count


def whole_of(shard):
    devices = lax.axis_size("fsdp")
    return jax.ShapeDtypeStruct((devices * shard.shape[0],) + shard.shape[1:], shard.dtype)


def gather_all(*shards):
    if lax.axis_size("fsdp") != 8:
        return tuple(lax.all_gather(shard, "fsdp", axis=0, tiled=True) for shard in shards)
    count = len(shards)
    return pl.pallas_call(
        functools.partial(gather_kernel, count),
        out_shape=tuple(whole_of(shard) for shard in shards),
        in_specs=anywhere(count),
        out_specs=tuple(anywhere(count)),
        scratch_shapes=[
            pltpu.SemaphoreType.DMA((count, 16)),
            pltpu.SemaphoreType.DMA((count, 16)),
            pltpu.SemaphoreType.DMA((count,)),
        ],
        compiler_params=pltpu.CompilerParams(collective_id=0, has_side_effects=True),
        name="gather_weights",
    )(*shards)


def gather_and_spread(grad_qkv, lowest):
    if lax.axis_size("fsdp") != 8 or lax.axis_size("section") < 2:
        lowest = jnp.where(lax.axis_index("section") == 0, lowest, jnp.zeros_like(lowest))
        input_grad = lax.psum(lowest, "section")
        return (
            lax.all_gather(grad_qkv, "fsdp", axis=0, tiled=True),
            input_grad,
            lax.all_gather(input_grad, "fsdp", axis=0, tiled=True),
        )
    return pl.pallas_call(
        spread_kernel,
        out_shape=(
            whole_of(grad_qkv),
            jax.ShapeDtypeStruct(lowest.shape, lowest.dtype),
            whole_of(lowest),
        ),
        in_specs=anywhere(2),
        out_specs=tuple(anywhere(3)),
        scratch_shapes=[
            pltpu.SemaphoreType.DMA((2, 16)),
            pltpu.SemaphoreType.DMA((2, 16)),
            pltpu.SemaphoreType.DMA((3,)),
            pltpu.SemaphoreType.DMA((CHUNKS,)),
            pltpu.SemaphoreType.DMA((CHUNKS,)),
        ],
        compiler_params=pltpu.CompilerParams(collective_id=1, has_side_effects=True),
        name="gather_gradients",
    )(grad_qkv, lowest)


def weight_kernel(split, normed_ref, qkv_ref, up_ref, att_ref, out_ref, normed_t, up_t):
    block = pl.program_id(0)

    @pl.when(block == 0)
    def _():
        normed_t[...] = normed_ref[...].T
        up_t[...] = up_ref[...].T

    @pl.when(block < split)
    def _():
        out_ref[0] = dot_nn(normed_t[...], qkv_ref[...])

    @pl.when(block >= split)
    def _():
        out_ref[0] = dot_nn(up_t[...], att_ref[...])


def weight_gradient(normed_columns, qkv_all, upstream_columns, attended_all):
    tokens, own = normed_columns.shape
    attn_width = attended_all.shape[1]
    if lax.axis_size("fsdp") != 8:
        parts = [dot_tn(normed_columns, qkv_all), dot_tn(upstream_columns, attended_all)]
        return jnp.concatenate(parts, axis=1)[None]
    split, total = 3 * attn_width // BLOCK, 4 * attn_width // BLOCK
    return pl.pallas_call(
        functools.partial(weight_kernel, split),
        grid=(total,),
        out_shape=jax.ShapeDtypeStruct((1, own, 4 * attn_width), jnp.float32),
        in_specs=[
            pl.BlockSpec((tokens, own), lambda j: (0, 0)),
            pl.BlockSpec((tokens, BLOCK), lambda j: (0, jnp.minimum(j, split - 1))),
            pl.BlockSpec((tokens, own), lambda j: (0, 0)),
            pl.BlockSpec((tokens, BLOCK), lambda j: (0, jnp.maximum(j - split, 0))),
        ],
        out_specs=pl.BlockSpec((1, own, BLOCK), lambda j: (0, 0, j)),
        scratch_shapes=[pltpu.VMEM((own, tokens), jnp.bfloat16)] * 2,
        compiler_params=pltpu.CompilerParams(vmem_limit_bytes=VMEM_LIMIT),
        cost_estimate=pl.CostEstimate(
            flops=8 * tokens * own * attn_width,
            bytes_accessed=8 * tokens * attn_width + 16 * own * attn_width,
            transcendentals=0,
        ),
        name="weight_gradient",
    )(normed_columns, qkv_all, upstream_columns, attended_all)


def on_device(saved_inputs, attn_weights, grad_out, segments, coords, embed_in, embed_out):
    section_count = lax.axis_size("section")
    section_index = lax.axis_index("section")
    micro_count, row_count, width = saved_inputs.shape[1:]
    attn_width = attn_weights.shape[2] // 4
    rows = micro_count * row_count
    placed = jnp.pad(coords.reshape(3, rows), ((0, 13), (0, -rows % 128)))
    weights, places = gather_all(attn_weights[0], placed)
    projection, output_weights = weights[:, : 3 * attn_width], weights[:, 3 * attn_width :]
    places = places.reshape(-1, 16, placed.shape[1])[:, :3, :rows]
    places = places.transpose(1, 0, 2).reshape(3, -1)
    augmented = jnp.concatenate([places, jnp.ones_like(places[:1])], axis=0)
    pre = jnp.dot(embed_in.astype(jnp.float32), augmented, precision=lax.Precision.HIGHEST)
    hidden, slope = gelu_value(pre).astype(jnp.bfloat16), gelu_slope(pre)

    values = saved_inputs[0].reshape(rows, width).astype(jnp.float32)
    norm_scale = lax.rsqrt(jnp.mean(values * values, axis=-1, keepdims=True) + EPS)
    normed = (values * norm_scale).astype(jnp.bfloat16)
    normed_columns = lax.all_to_all(normed, "fsdp", split_axis=1, concat_axis=0, tiled=True)
    micro = lax.broadcasted_iota(jnp.int32, (micro_count, row_count), 0)
    row_id = (segments[:, 0, :] + micro * 1024).reshape(rows)

    qkv = dot_nn(normed, projection).astype(jnp.bfloat16)
    prob, attended = attention_forward(qkv, row_id)
    attended_all = lax.all_gather(attended, "fsdp", axis=0, tiled=True)

    chunk = width // CHUNKS
    cuts = [slice(c * chunk, (c + 1) * chunk) for c in range(CHUNKS)]
    is_top = section_index == section_count - 1
    top = grad_out.reshape(rows, width)
    top = jnp.where(is_top, top, jnp.zeros_like(top))
    from_top = dot_nn(top, output_weights)
    down = [(i, i - 1) for i in range(1, section_count)]
    upstream, grad_attended = [top[:, cut] for cut in cuts], from_top
    for step in range(section_count):
        if step > 0:
            upstream = [received[c] + top[:, cuts[c]] for c in range(CHUNKS)]
            grad_attended = from_top
            for c in range(CHUNKS):
                grad_attended = grad_attended + dot_nn(received[c], output_weights[cuts[c]])
        grad_qkv, row_sum = attention_backward(qkv, grad_attended.astype(jnp.bfloat16), prob)
        shrink = norm_scale * norm_scale * row_sum / width
        received, grad_inputs = [], []
        for c in range(CHUNKS):
            fresh = (
                upstream[c].astype(jnp.float32)
                + norm_scale * dot_nt(grad_qkv, projection[cuts[c]])
                - values[:, cuts[c]] * shrink
            ).astype(jnp.bfloat16)
            grad_inputs.append(fresh)
            if step < section_count - 1:
                received.append(lax.ppermute(fresh, "section", down))

    upstream_columns = lax.all_to_all(
        jnp.concatenate(upstream, axis=1), "fsdp", split_axis=1, concat_axis=0, tiled=True
    )
    lowest = jnp.concatenate(grad_inputs, axis=1)
    if lax.axis_size("fsdp") == 8:
        lowest, upstream_columns = lax.optimization_barrier((lowest, upstream_columns))
    qkv_all, input_grad, input_all = gather_and_spread(grad_qkv, lowest)
    attn_grad = weight_gradient(normed_columns, qkv_all, upstream_columns, attended_all)
    embed_out_grad = dot_nn(hidden, input_all)
    grad_pre = dot_nt(embed_out, input_all) * slope
    embed_in_grad = lax.dot_general(
        grad_pre, augmented, (((1,), (1,)), ((), ())), precision=lax.Precision.HIGHEST
    )
    return (
        attn_grad,
        input_grad.reshape(micro_count, row_count, width),
        embed_out_grad,
        embed_in_grad,
    )


def solution(mesh):
    placed = (
        P("section", None, "fsdp", None),
        P("section", "fsdp", None),
        P(None, "fsdp", None),
        P(None, "fsdp", None),
        P(None, None, "fsdp"),
        P(("section", "fsdp"), None),
        P(("section", "fsdp"), None),
    )
    return jax.shard_map(
        on_device,
        mesh=mesh,
        in_specs=placed,
        out_specs=(
            P("section", "fsdp", None),
            P(None, "fsdp", None),
            P(("section", "fsdp"), None),
            P(("section", "fsdp"), None),
        ),
        check_vma=False,
    )
```

```python
import functools

import jax
import jax.numpy as jnp
from jax import lax
from jax.experimental import pallas as pl
from jax.experimental.pallas import tpu as pltpu
from jax.sharding import PartitionSpec as P

HEAD_DIM = 64
PAIR = 2 * HEAD_DIM
EPS = 1e-05
CHUNKS = 4
MESH = pl.DeviceIdType.MESH
VMEM_LIMIT = 40 * 1024 * 1024


def gelu_value(pre):
    return 0.5 * pre * (1.0 + jax.scipy.special.erf(pre / jnp.sqrt(2.0)))


def gelu_slope(pre):
    return 0.5 * (1.0 + jax.scipy.special.erf(pre / jnp.sqrt(2.0))) + pre * jnp.exp(
        -0.5 * pre * pre
    ) / jnp.sqrt(2.0 * jnp.pi)


def dot_nt(left, right):
    return lax.dot_general(
        left, right, (((1,), (1,)), ((), ())), preferred_element_type=jnp.float32
    )


def dot_tn(left, right):
    return lax.dot_general(
        left, right, (((0,), (0,)), ((), ())), preferred_element_type=jnp.float32
    )


def dot_nn(left, right):
    return jnp.dot(left, right, preferred_element_type=jnp.float32)


def half_masks(rows):
    low = lax.broadcasted_iota(jnp.int32, (rows, PAIR), 1) < HEAD_DIM
    return low


def forward_kernel(attn_width, qkv_ref, row_id_ref, col_id_ref, prob_ref, att_ref):
    rows = qkv_ref.shape[0]
    same = row_id_ref[...] == col_id_ref[...]
    low = half_masks(rows)
    zero = jnp.zeros((rows, PAIR), jnp.bfloat16)
    for pair in range(attn_width // PAIR):
        at = pair * PAIR
        query = qkv_ref[:, at : at + PAIR]
        key = qkv_ref[:, attn_width + at : attn_width + at + PAIR]
        value = qkv_ref[:, 2 * attn_width + at : 2 * attn_width + at + PAIR]
        parts = []
        for half in range(2):
            mine = low if half == 0 else jnp.logical_not(low)
            scores = dot_nt(jnp.where(mine, key, zero), query) * (HEAD_DIM**-0.5)
            scores = jnp.where(same, scores, -1e30)
            exponent = jnp.exp(scores - jnp.max(scores, axis=0, keepdims=True))
            prob = exponent / jnp.sum(exponent, axis=0, keepdims=True)
            prob_ref[2 * pair + half] = prob
            parts.append(dot_tn(prob.astype(jnp.bfloat16), value))
        att_ref[:, at : at + PAIR] = jnp.where(low, parts[0], parts[1]).astype(jnp.bfloat16)


def backward_kernel(attn_width, qkv_ref, up_ref, prob_ref, out_ref, sum_ref):
    rows = qkv_ref.shape[0]
    low = half_masks(rows)
    zero = jnp.zeros((rows, PAIR), jnp.bfloat16)
    total = jnp.zeros((rows, PAIR), jnp.float32)
    for pair in range(attn_width // PAIR):
        at = pair * PAIR
        query = qkv_ref[:, at : at + PAIR]
        key = qkv_ref[:, attn_width + at : attn_width + at + PAIR]
        value = qkv_ref[:, 2 * attn_width + at : 2 * attn_width + at + PAIR]
        up = up_ref[:, at : at + PAIR]
        parts = []
        for half in range(2):
            mine = low if half == 0 else jnp.logical_not(low)
            prob = prob_ref[2 * pair + half]
            grad_prob = dot_nt(jnp.where(mine, value, zero), up)
            delta = jnp.sum(prob * grad_prob, axis=0, keepdims=True)
            grad_score = (prob * (grad_prob - delta) * (HEAD_DIM**-0.5)).astype(jnp.bfloat16)
            parts.append(
                (
                    dot_tn(grad_score, key),
                    dot_nn(grad_score, query),
                    dot_nn(prob.astype(jnp.bfloat16), up),
                )
            )
        for place, own in enumerate((query, key, value)):
            grad = jnp.where(low, parts[0][place], parts[1][place]).astype(jnp.bfloat16)
            left = place * attn_width + at
            out_ref[:, left : left + PAIR] = grad
            total = total + own.astype(jnp.float32) * grad.astype(jnp.float32)
    sum_ref[...] = jnp.sum(total, axis=1, keepdims=True)


def whole_vmem(count):
    return [pl.BlockSpec(memory_space=pltpu.VMEM)] * count


def attention_forward(qkv, row_id):
    rows, attn_width = qkv.shape[0], qkv.shape[1] // 3
    heads = attn_width // HEAD_DIM
    return pl.pallas_call(
        functools.partial(forward_kernel, attn_width),
        out_shape=(
            jax.ShapeDtypeStruct((heads, rows, rows), jnp.float32),
            jax.ShapeDtypeStruct((rows, attn_width), jnp.bfloat16),
        ),
        in_specs=whole_vmem(3),
        out_specs=tuple(whole_vmem(2)),
        compiler_params=pltpu.CompilerParams(vmem_limit_bytes=VMEM_LIMIT),
        cost_estimate=pl.CostEstimate(
            flops=4 * rows * rows * attn_width,
            bytes_accessed=8 * rows * attn_width + 4 * heads * rows * rows,
            transcendentals=heads * rows * rows,
        ),
        name="attention_forward",
    )(qkv, row_id.reshape(rows, 1), row_id.reshape(1, rows))


def attention_backward(qkv, up, prob):
    rows, attn_width = qkv.shape[0], qkv.shape[1] // 3
    heads = attn_width // HEAD_DIM
    return pl.pallas_call(
        functools.partial(backward_kernel, attn_width),
        out_shape=(
            jax.ShapeDtypeStruct((rows, 3 * attn_width), jnp.bfloat16),
            jax.ShapeDtypeStruct((rows, 1), jnp.float32),
        ),
        in_specs=whole_vmem(3),
        out_specs=tuple(whole_vmem(2)),
        compiler_params=pltpu.CompilerParams(vmem_limit_bytes=VMEM_LIMIT),
        cost_estimate=pl.CostEstimate(
            flops=8 * rows * rows * attn_width,
            bytes_accessed=14 * rows * attn_width + 4 * heads * rows * rows,
            transcendentals=0,
        ),
        name="attention_backward",
    )(qkv, up, prob)


def gather_plan(shard_ref, out_ref, send_sems, recv_sems, local_sem):
    section, me = lax.axis_index("section"), lax.axis_index("fsdp")
    core, first, second = me % 2, (me // 2) % 2, me // 4
    rows = shard_ref.shape[0]
    half_rows = rows // 2

    def device(bits):
        other_core = core + (1 - 2 * core) * (bits % 2)
        other_first = first + (1 - 2 * first) * (bits // 2 % 2)
        other_second = second + (1 - 2 * second) * (bits // 4)
        return other_second * 4 + other_first * 2 + other_core

    def place(bits, half):
        start = pl.multiple_of(device(bits) * rows + half * half_rows, half_rows)
        return out_ref.at[pl.ds(start, half_rows)]

    def copy(bits, half, to):
        source = shard_ref.at[pl.ds(half * half_rows, half_rows)] if bits == 0 else place(bits, half)
        arrives = bits + to
        return pltpu.make_async_remote_copy(
            src_ref=source,
            dst_ref=place(bits, half),
            send_sem=send_sems.at[arrives * 2 + half],
            recv_sem=recv_sems.at[arrives * 2 + half],
            device_id=(section, device(to)),
            device_id_type=MESH,
        )

    def arrived(bits, half):
        pltpu.make_async_remote_copy(
            src_ref=place(bits, half),
            dst_ref=place(bits, half),
            send_sem=send_sems.at[bits * 2 + half],
            recv_sem=recv_sems.at[bits * 2 + half],
            device_id=(section, device(1)),
            device_id_type=MESH,
        ).wait_recv()

    started = []

    def send(bits, half, to):
        each = copy(bits, half, to)
        each.start()
        started.append(each)

    own = pltpu.make_async_copy(
        shard_ref, out_ref.at[pl.ds(pl.multiple_of(me * rows, rows), rows)], local_sem
    )

    def begin():
        send(0, 0, 2)
        send(0, 1, 4)
        send(0, 0, 4)
        send(0, 1, 2)
        send(0, 0, 1)
        send(0, 1, 1)
        own.start()

    def relay():
        arrived(2, 0)
        send(2, 0, 4)
        send(2, 0, 1)
        arrived(4, 1)
        send(4, 1, 2)
        send(4, 1, 1)

    def hand_over():
        for bits, half in ((4, 0), (2, 1), (6, 0), (6, 1)):
            arrived(bits, half)
            send(bits, half, 1)

    def finish():
        for bits in (1, 3, 5, 7):
            arrived(bits, 0)
            arrived(bits, 1)
        for each in started:
            each.wait_send()
        own.wait()

    return begin, relay, hand_over, finish


def greet(along_section):
    section, me = lax.axis_index("section"), lax.axis_index("fsdp")
    core, first, second = me % 2, (me // 2) % 2, me // 4
    barrier = pltpu.get_barrier_semaphore()
    for other in (me + 1 - 2 * core, me + 2 * (1 - 2 * first), me + 4 * (1 - 2 * second)):
        pl.semaphore_signal(barrier, inc=1, device_id=(section, other), device_id_type=MESH)
    if not along_section:
        pl.semaphore_wait(barrier, 3)
        return
    last = lax.axis_size("section") - 1

    @pl.when(section > 0)
    def _():
        pl.semaphore_signal(barrier, inc=1, device_id=(section - 1, me), device_id_type=MESH)

    @pl.when(section < last)
    def _():
        pl.semaphore_signal(barrier, inc=1, device_id=(section + 1, me), device_id_type=MESH)

    @pl.when(jnp.logical_or(section == 0, section == last))
    def _():
        pl.semaphore_wait(barrier, 4)

    @pl.when(jnp.logical_and(section > 0, section < last))
    def _():
        pl.semaphore_wait(barrier, 5)


def gather_kernel(count, *refs):
    shards, outs, (send_sems, recv_sems, local_sems) = refs[:count], refs[count : 2 * count], refs[2 * count :]
    greet(False)
    plans = [
        gather_plan(shards[i], outs[i], send_sems.at[i], recv_sems.at[i], local_sems.at[i])
        for i in range(count)
    ]
    for stage in range(4):
        for plan in plans:
            plan[stage]()


def spread_kernel(
    qkv_ref, low_ref, qkv_all_ref, own_ref, all_ref, send_sems, recv_sems, local_sems, up_send, up_recv
):
    section, me = lax.axis_index("section"), lax.axis_index("fsdp")
    last = lax.axis_size("section") - 1
    chunk = low_ref.shape[0] // CHUNKS
    greet(True)
    first = gather_plan(qkv_ref, qkv_all_ref, send_sems.at[0], recv_sems.at[0], local_sems.at[0])
    second = gather_plan(own_ref, all_ref, send_sems.at[1], recv_sems.at[1], local_sems.at[1])
    keep = pltpu.make_async_copy(low_ref, own_ref, local_sems.at[2])

    def upward(source, c):
        cut = pl.ds(c * chunk, chunk)
        return pltpu.make_async_remote_copy(
            src_ref=source.at[cut],
            dst_ref=own_ref.at[cut],
            send_sem=up_send.at[c],
            recv_sem=up_recv.at[c],
            device_id=(jnp.minimum(section + 1, last), me),
            device_id_type=MESH,
        )

    @pl.when(section == 0)
    def _():
        for c in range(CHUNKS):
            upward(low_ref, c).start()
        keep.start()

    first[0]()

    @pl.when(section == 0)
    def _():
        keep.wait()

    for c in range(CHUNKS):

        @pl.when(section > 0)
        def _():
            upward(own_ref, c).wait_recv()

        @pl.when(jnp.logical_and(section > 0, section < last))
        def _():
            upward(own_ref, c).start()

    first[1]()
    second[0]()
    first[2]()
    second[1]()
    second[2]()
    first[3]()
    second[3]()

    @pl.when(section < last)
    def _():
        for c in range(CHUNKS):
            upward(own_ref, c).wait_send()


def anywhere(count):
    return [pl.BlockSpec(memory_space=pl.ANY)] * count


def whole_of(shard):
    devices = lax.axis_size("fsdp")
    return jax.ShapeDtypeStruct((devices * shard.shape[0],) + shard.shape[1:], shard.dtype)


def gather_all(*shards):
    if lax.axis_size("fsdp") != 8:
        return tuple(lax.all_gather(shard, "fsdp", axis=0, tiled=True) for shard in shards)
    count = len(shards)
    return pl.pallas_call(
        functools.partial(gather_kernel, count),
        out_shape=tuple(whole_of(shard) for shard in shards),
        in_specs=anywhere(count),
        out_specs=tuple(anywhere(count)),
        scratch_shapes=[
            pltpu.SemaphoreType.DMA((count, 16)),
            pltpu.SemaphoreType.DMA((count, 16)),
            pltpu.SemaphoreType.DMA((count,)),
        ],
        compiler_params=pltpu.CompilerParams(collective_id=0, has_side_effects=True),
        name="gather_weights",
    )(*shards)


def gather_and_spread(grad_qkv, lowest):
    if lax.axis_size("fsdp") != 8 or lax.axis_size("section") < 2:
        lowest = jnp.where(lax.axis_index("section") == 0, lowest, jnp.zeros_like(lowest))
        input_grad = lax.psum(lowest, "section")
        return (
            lax.all_gather(grad_qkv, "fsdp", axis=0, tiled=True),
            input_grad,
            lax.all_gather(input_grad, "fsdp", axis=0, tiled=True),
        )
    return pl.pallas_call(
        spread_kernel,
        out_shape=(
            whole_of(grad_qkv),
            jax.ShapeDtypeStruct(lowest.shape, lowest.dtype),
            whole_of(lowest),
        ),
        in_specs=anywhere(2),
        out_specs=tuple(anywhere(3)),
        scratch_shapes=[
            pltpu.SemaphoreType.DMA((2, 16)),
            pltpu.SemaphoreType.DMA((2, 16)),
            pltpu.SemaphoreType.DMA((3,)),
            pltpu.SemaphoreType.DMA((CHUNKS,)),
            pltpu.SemaphoreType.DMA((CHUNKS,)),
        ],
        compiler_params=pltpu.CompilerParams(collective_id=1, has_side_effects=True),
        name="gather_gradients",
    )(grad_qkv, lowest)


def on_device(saved_inputs, attn_weights, grad_out, segments, coords, embed_in, embed_out):
    section_count = lax.axis_size("section")
    section_index = lax.axis_index("section")
    micro_count, row_count, width = saved_inputs.shape[1:]
    attn_width = attn_weights.shape[2] // 4
    rows = micro_count * row_count
    placed = jnp.pad(coords.reshape(3, rows), ((0, 13), (0, -rows % 128)))
    weights, places = gather_all(attn_weights[0], placed)
    projection, output_weights = weights[:, : 3 * attn_width], weights[:, 3 * attn_width :]
    places = places.reshape(-1, 16, placed.shape[1])[:, :3, :rows]
    places = places.transpose(1, 0, 2).reshape(3, -1)
    augmented = jnp.concatenate([places, jnp.ones_like(places[:1])], axis=0)
    pre = jnp.dot(embed_in.astype(jnp.float32), augmented, precision=lax.Precision.HIGHEST)
    hidden, slope = gelu_value(pre).astype(jnp.bfloat16), gelu_slope(pre)

    values = saved_inputs[0].reshape(rows, width).astype(jnp.float32)
    norm_scale = lax.rsqrt(jnp.mean(values * values, axis=-1, keepdims=True) + EPS)
    normed = (values * norm_scale).astype(jnp.bfloat16)
    normed_columns = lax.all_to_all(normed, "fsdp", split_axis=1, concat_axis=0, tiled=True)
    micro = lax.broadcasted_iota(jnp.int32, (micro_count, row_count), 0)
    row_id = (segments[:, 0, :] + micro * 1024).reshape(rows)

    qkv = dot_nn(normed, projection).astype(jnp.bfloat16)
    prob, attended = attention_forward(qkv, row_id)
    attended_all = lax.all_gather(attended, "fsdp", axis=0, tiled=True)

    chunk = width // CHUNKS
    cuts = [slice(c * chunk, (c + 1) * chunk) for c in range(CHUNKS)]
    is_top = section_index == section_count - 1
    top = grad_out.reshape(rows, width)
    top = jnp.where(is_top, top, jnp.zeros_like(top))
    from_top = dot_nn(top, output_weights)
    down = [(i, i - 1) for i in range(1, section_count)]
    upstream, grad_attended = [top[:, cut] for cut in cuts], from_top
    for step in range(section_count):
        if step > 0:
            upstream = [received[c] + top[:, cuts[c]] for c in range(CHUNKS)]
            grad_attended = from_top
            for c in range(CHUNKS):
                grad_attended = grad_attended + dot_nn(received[c], output_weights[cuts[c]])
        grad_qkv, row_sum = attention_backward(qkv, grad_attended.astype(jnp.bfloat16), prob)
        if step == 1 and lax.axis_size("fsdp") == 8:
            grad_qkv, normed_columns = lax.optimization_barrier((grad_qkv, normed_columns))
        shrink = norm_scale * norm_scale * row_sum / width
        received, grad_inputs = [], []
        for c in range(CHUNKS):
            fresh = (
                upstream[c].astype(jnp.float32)
                + norm_scale * dot_nt(grad_qkv, projection[cuts[c]])
                - values[:, cuts[c]] * shrink
            ).astype(jnp.bfloat16)
            grad_inputs.append(fresh)
            if step < section_count - 1:
                received.append(lax.ppermute(fresh, "section", down))

    upstream_columns = lax.all_to_all(
        jnp.concatenate(upstream, axis=1), "fsdp", split_axis=1, concat_axis=0, tiled=True
    )
    lowest = jnp.concatenate(grad_inputs, axis=1)
    if lax.axis_size("fsdp") == 8:
        lowest, upstream_columns = lax.optimization_barrier((lowest, upstream_columns))
    qkv_all, input_grad, input_all = gather_and_spread(grad_qkv, lowest)
    attn_grad = jnp.concatenate(
        [dot_tn(normed_columns, qkv_all), dot_tn(upstream_columns, attended_all)], axis=1
    )
    embed_out_grad = dot_nn(hidden, input_all)
    grad_pre = dot_nt(embed_out, input_all) * slope
    embed_in_grad = lax.dot_general(
        grad_pre, augmented, (((1,), (1,)), ((), ())), precision=lax.Precision.HIGHEST
    )
    return (
        attn_grad[None],
        input_grad.reshape(micro_count, row_count, width),
        embed_out_grad,
        embed_in_grad,
    )


def solution(mesh):
    placed = (
        P("section", None, "fsdp", None),
        P("section", "fsdp", None),
        P(None, "fsdp", None),
        P(None, "fsdp", None),
        P(None, None, "fsdp"),
        P(("section", "fsdp"), None),
        P(("section", "fsdp"), None),
    )
    return jax.shard_map(
        on_device,
        mesh=mesh,
        in_specs=placed,
        out_specs=(
            P("section", "fsdp", None),
            P(None, "fsdp", None),
            P(("section", "fsdp"), None),
            P(("section", "fsdp"), None),
        ),
        check_vma=False,
    )
```
